256 devices in a mesh: blk: 64 (over x, y, z_hi), rep: 4 (over z_lo, core).
Axes of the slice: x: 4, y: 4, z: 8 (z_hi: 4, z_lo: 2; z = z_hi * 2 + z_lo), core: 2. Of those that a mesh axis runs over, the one named last changes fastest.
Arguments:
- row_embed: float32 [131072, 300], P(('blk', 'rep')), may hold values from -1.5 to 1.5
- col_embed: float32 [131072, 300], P(('blk', 'rep')), may hold values from -1.5 to 1.5
- counts: int32 [2, 131072, 2048], P(None, ('blk', 'rep')), may hold values from 0 to 199, as said below
- log_marginal: float32 [131072], replicated, may hold values from 8 to 12
Outputs:
- rows_after: float32 [131072, 300], P(('blk', 'rep'))
- cols_after: float32 [131072, 300], P(('blk', 'rep'))
The draws below stay inside these ranges and needn't reach their ends.
Inputs may be any that keep to these rules, and one draw needn't show every extreme that they name: About half the counts are zero; the rest are spread evenly.
All inputs are finite; a program needn't handle non-finite values.
Results may differ from the reference program's by a relative error of at most 0.0029.
Values may be sent and summed in bfloat16 or wider, within the bound.
A program may use at most 64 MiB of HBM per device.

```python
import jax
import jax.numpy as jnp
from jax import lax

W = 300
BLOCK = 2048
ROUNDS = 2
NROWS = 131072
N_BLK = 64


def draw_counts(key, part):
    key = jax.random.fold_in(key, 7)
    first, second = jax.random.split(key)
    shape = (ROUNDS, NROWS, BLOCK)
    values = jax.random.randint(first, shape, 1, 200, dtype=jnp.int32)
    keeper = jax.random.randint(second, shape, 0, 2, dtype=jnp.int32)
    return values * keeper


def shard_levels(stream_key, extent, cuts, low, largest):
    def one(dim, parts):
        draws = jax.random.uniform(jax.random.fold_in(jax.random.fold_in(stream_key, 6), dim), (parts,), jnp.float32, low / len(cuts), largest / len(cuts))
        return jnp.repeat(jnp.exp(draws), extent[dim] // parts).reshape((-1,) + (1,) * (len(extent) - dim - 1))

    loudness = one(*cuts[0])
    for cut in cuts[1:]:
        loudness = loudness * one(*cut)
    return loudness


def normal_values(stream_key, dims, spread, most, shards=(), held_as=jnp.bfloat16):
    values = jax.random.normal(stream_key, dims, jnp.float32) * spread
    if len(shards) > 0:
        values = shard_levels(stream_key, dims, shards, -0.22, 0.18) * values
    return jnp.clip(values, min=-most, max=most).astype(held_as)


def setup_inputs(seed: int = 0) -> dict:
    splits = jax.random.split(jax.random.key(seed), 5)
    return {
        "row_embed": normal_values(splits[0], (NROWS, W), 0.25, 1.5, ((0, 256),), jnp.float32),
        "col_embed": normal_values(splits[1], (NROWS, W), 0.25, 1.5, ((0, 256),), jnp.float32),
        "counts": draw_counts(jax.random.fold_in(splits[4], 71), 0),
        "log_marginal": jnp.clip(jax.random.uniform(splits[3], (NROWS,), jnp.float32, 8.0, 12.0), 8.0, 12.0),
    }


step_size = 0.05

def slope_of(pred, count_int, pmi, scale):
    count = count_int.astype(jnp.float32)
    confidence = 0.1 + 0.25 * jnp.sqrt(count)
    target = jnp.log(jnp.maximum(count, 1.0)) + pmi
    slope = jnp.where(count_int > 0, confidence * (pred - target), jax.nn.sigmoid(pred - pmi))
    return (slope * scale).astype(jnp.bfloat16)

def fit_round(rows, cols, tile_counts, log_marginal, log_total, swap_bit):
    blocks = rows.shape[0] // BLOCK
    order = jnp.bitwise_xor(jnp.arange(blocks, dtype=jnp.int32), 1 << swap_bit)
    row_half = rows.astype(jnp.bfloat16).reshape(blocks, BLOCK, W)
    col_half = cols.astype(jnp.bfloat16).reshape(blocks, BLOCK, W)[order]
    margin = log_marginal.reshape(blocks, BLOCK)
    tiles = tile_counts.reshape(blocks, BLOCK, BLOCK)
    scale = 1.0 / jnp.sqrt(jnp.float32(BLOCK))

    def one_block(items):
        left, right, tile, row_margin, col_margin = items
        pred = jnp.dot(left, right.T, preferred_element_type=jnp.float32)
        pmi = log_total - row_margin[:, None] - col_margin[None, :]
        slope = slope_of(pred, tile, pmi, scale)
        row_grad = jnp.dot(slope, right, preferred_element_type=jnp.float32)
        col_grad = jnp.dot(slope.T, left, preferred_element_type=jnp.float32)
        return (row_grad, col_grad)
    row_grad, far_grad = lax.map(one_block, (row_half, col_half, tiles, margin, margin[order]))
    col_grad = far_grad[order]
    return (row_grad.reshape(-1, W), col_grad.reshape(-1, W))

def reference(row_embed, col_embed, counts, log_marginal):
    log_total = jax.nn.logsumexp(log_marginal)
    rows, cols = (row_embed, col_embed)
    bits = [N_BLK.bit_length() - 2, 0]
    for rnd in range(ROUNDS):
        row_grad, col_grad = fit_round(rows, cols, counts[rnd], log_marginal, log_total, bits[rnd])
        rows = rows - step_size * row_grad
        cols = cols - step_size * col_grad
    return (rows, cols)
```

```python
import functools

import jax
import jax.numpy as jnp
from jax import lax
from jax.experimental import pallas as pl
from jax.experimental.pallas import tpu as pltpu
from jax.sharding import PartitionSpec as P

STEP = 0.05
PARTS = 4
CUTS = 4
MESH = pl.DeviceIdType.MESH
TO_PARTNER, TO_CORE, TO_NEAR, TO_CORE_FAR, PART_A, PART_B, SUM_NEAR, SUM_NEAR_FAR, TOTAL, TOTAL_FAR, TO_NEAR_FAR = range(11)
KINDS = 11


def other(bit):
    return 1 - bit


def kernel(
    n_blk, rounds, cuts, piece,
    rows_ref, cols_ref, counts_ref, margin_ref, rows_out, cols_out,
    counts, gain, shift, rows_f, rows_t, rows_n, row_grad, cols_f, row_margin,
    sent, came, part_own, part_out, part_in, near_out, near_in, total_out, total_in,
    count_sem, send_sem, came_sem, part_sem, near_sem, total_sem,
):
    width, local = rows_ref.shape
    padded = rows_f.shape[0]
    pieces = rounds * cuts
    blk = lax.axis_index("blk")
    rep = lax.axis_index("rep")
    near = rep // 2
    core = rep % 2
    high = n_blk // 2
    inner = (blk + near) % 2 == 1
    outer = (blk + near) % 2 == 0
    across = (blk + high) % n_blk
    along = blk + 1 - 2 * (blk % 2)
    core_id = (blk, near * 2 + other(core))
    near_id = (blk, other(near) * 2 + core)
    across_id = (across, rep)
    along_id = (along, rep)
    touch_id = (along, other(near) * 2 + core)

    barrier = pltpu.get_barrier_semaphore()
    for partner in (core_id, near_id, across_id, along_id, touch_id):
        pl.semaphore_signal(barrier, inc=1, device_id=partner, device_id_type=MESH)

    def part_of(d):
        return ((near + d // 2) % 2) * 2 + (core + d % 2) % 2

    def count_copy(rnd, d):
        start = pl.multiple_of(part_of(d) * local, local)
        return pltpu.make_async_copy(
            counts_ref.at[rnd, :, pl.ds(start, local)], counts.at[rnd * PARTS + d], count_sem.at[rnd * PARTS + d]
        )

    for rnd in range(rounds):
        for d in range(PARTS):
            count_copy(rnd, d).start()

    def send(kind, g, src, dst, sem, target):
        pltpu.make_async_remote_copy(
            src_ref=src, dst_ref=dst, send_sem=send_sem.at[kind, g], recv_sem=sem, device_id=target, device_id_type=MESH
        ).start()

    def landed(ref, sem):
        pltpu.make_async_copy(ref, ref, sem).wait()

    def lanes(j):
        return pl.ds(pl.multiple_of(j * piece, piece), piece)

    cols_f[width:, :] = jnp.zeros((padded - width, local), jnp.float32)
    cols_f[:width, :] = cols_ref[...]
    rows_f[width:, :] = jnp.zeros((padded - width, local), jnp.float32)
    rows_f[:width, :] = rows_ref[...]

    def send_cols(g, rnd):
        sent[g] = cols_f[:, lanes(g % cuts)].astype(jnp.bfloat16)

    for j in range(cuts):
        sent[j] = cols_f[:, j * piece : (j + 1) * piece].astype(jnp.bfloat16)
    pl.semaphore_wait(barrier, 5)
    for j in range(cuts):
        send(TO_PARTNER, j, sent.at[j], came.at[0, j], came_sem.at[0, j], across_id)

    def set_rows():
        rows = rows_f[...]
        rows_t[...] = rows.astype(jnp.bfloat16)
        rows_n[...] = rows.T.astype(jnp.bfloat16)
        row_grad[...] = jnp.zeros_like(row_grad)

    set_rows()
    margins = margin_ref[...]
    most = jnp.max(jnp.max(margins, axis=0, keepdims=True), axis=1, keepdims=True)
    mass = jnp.sum(jnp.sum(jnp.exp(margins - most), axis=0, keepdims=True), axis=1, keepdims=True)
    log_total = jnp.log(mass) + most
    lines = local // 128
    for k in range(lines):
        line = margin_ref[pl.ds((blk * PARTS + rep) * lines + k, 1), :]
        row_margin[k * 128 : (k + 1) * 128, :] = jnp.broadcast_to(line, (128, 128)).T - log_total

    scale = float(1.0 / (PARTS * local) ** 0.5)

    def prepare(g, d):
        rnd, j = g // cuts, g % cuts
        partner = across + rnd * (along - across)
        first = (partner * PARTS + part_of(d)) * lines + j * (piece // 128)

        @pl.when(j == 0)
        def _():
            count_copy(rnd, d).wait()

        for h in range(piece // 128):
            number = counts[rnd * PARTS + d, :, pl.ds(pl.multiple_of(j * piece + h * 128, 128), 128)]
            count = number.astype(jnp.float32)
            least = jnp.maximum(count, 1.0)
            confidence = scale * 0.1 + (scale * 0.25) * (count * lax.rsqrt(least))
            gain[g * PARTS + d, :, h * 128 : (h + 1) * 128] = jnp.where(number > 0, confidence, -0.5)
            shift[g * PARTS + d, :, h * 128 : (h + 1) * 128] = (
                row_margin[...] + margin_ref[pl.ds(first + h, 1), :]
            ) - jnp.log(least)

    def compute(g, d):
        block = came[d, g]
        pred = jnp.dot(rows_n[...], block, preferred_element_type=jnp.float32)
        factor = gain[g * PARTS + d]
        value = factor * (pred + shift[g * PARTS + d])
        smooth = (0.5 * scale) - (0.5 * scale) * jnp.tanh(value)
        slope = jnp.where(factor > 0.0, value, smooth).astype(jnp.bfloat16)
        far = jnp.dot(rows_t[...], slope, preferred_element_type=jnp.float32)
        row_grad[...] += lax.dot_general(block, slope, (((1,), (1,)), ((), ())), preferred_element_type=jnp.float32)
        if d % 2 == 0:
            part_own[d // 2, g] = far
        else:
            part_out[d // 2, g] = far.astype(jnp.bfloat16)
            send(PART_A + d // 2, g, part_out.at[d // 2, g], part_in.at[d // 2, g], part_sem.at[d // 2, g], core_id)

    def pass_first(g):
        landed(came.at[0, g], came_sem.at[0, g])
        send(TO_CORE, g, came.at[0, g], came.at[1, g], came_sem.at[1, g], core_id)

        @pl.when((g < cuts) | inner)
        def _():
            send(TO_NEAR, g, came.at[0, g], came.at[2, g], came_sem.at[2, g], near_id)

    def pass_second(g):
        landed(came.at[2, g], came_sem.at[2, g])
        send(TO_CORE_FAR, g, came.at[2, g], came.at[3, g], came_sem.at[3, g], core_id)

        @pl.when((g >= cuts) & inner)
        def _():
            send(TO_NEAR_FAR, g, came.at[2, g], came.at[0, g], came_sem.at[0, g], near_id)

    def chip_sum(g, k):
        landed(part_in.at[k, g], part_sem.at[k, g])
        return part_own[k, g] + part_in[k, g].astype(jnp.float32)

    def reduce_near(g):
        @pl.when((g < cuts) | outer)
        def _():
            near_out[0, g] = chip_sum(g, 1).astype(jnp.bfloat16)
            send(SUM_NEAR, g, near_out.at[0, g], near_in.at[0, g], near_sem.at[0, g], near_id)

        @pl.when((g >= cuts) & outer)
        def _():
            near_out[1, g] = chip_sum(g, 0).astype(jnp.bfloat16)
            send(SUM_NEAR_FAR, g, near_out.at[1, g], near_in.at[1, g], near_sem.at[1, g], near_id)

    def both_sum(g, k):
        own = chip_sum(g, k)
        landed(near_in.at[k, g], near_sem.at[k, g])
        return (own + near_in[k, g].astype(jnp.float32)).astype(jnp.bfloat16)

    def reduce_far(g):
        rnd = g // cuts

        @pl.when((g < cuts) | inner)
        def _():
            total_out[0, g] = both_sum(g, 0)
            send(
                TOTAL, g, total_out.at[0, g], total_in.at[g], total_sem.at[g], (across + rnd * (along - across), rep)
            )

        @pl.when((g >= cuts) & inner)
        def _():
            total_out[1, g] = both_sum(g, 1)
            send(TOTAL_FAR, g, total_out.at[1, g], total_in.at[g], total_sem.at[g], touch_id)

    def finish(g):
        j = g % cuts
        landed(total_in.at[g], total_sem.at[g])
        new = cols_f[:, lanes(j)] - STEP * total_in[g].astype(jnp.float32)
        cols_f[:, lanes(j)] = new

        @pl.when(g < pieces - cuts)
        def _():
            later = g + cuts
            sent[later] = new.astype(jnp.bfloat16)

            @pl.when(outer)
            def _():
                send(TO_PARTNER, later, sent.at[later], came.at[0, later], came_sem.at[0, later], along_id)

            @pl.when(inner)
            def _():
                send(TO_PARTNER, later, sent.at[later], came.at[2, later], came_sem.at[2, later], touch_id)

    pass_first(0)
    for d in range(PARTS):
        prepare(0, d)
    pass_second(0)

    def body(g, carry):
        @pl.when(g == cuts)
        def _():
            rows_f[...] = rows_f[...] - STEP * row_grad[...]
            set_rows()

        for d in range(PARTS):
            @pl.when(g < pieces)
            def _():
                if d % 2 == 1:
                    landed(came.at[d, g], came_sem.at[d, g])
                compute(g, d)

            if d == 1:
                @pl.when((g >= 1) & (g <= pieces))
                def _():
                    reduce_near(g - 1)

                @pl.when(g + 1 < cuts)
                def _():
                    pass_first(g + 1)

            @pl.when(g + 1 < pieces)
            def _():
                prepare(g + 1, d)

        @pl.when(g + 1 < cuts)
        def _():
            pass_second(g + 1)

        @pl.when((g >= 1) & (g <= pieces))
        def _():
            reduce_far(g - 1)

        @pl.when(g >= 2)
        def _():
            finish(g - 2)

        @pl.when((g + 1 >= cuts) & (g + 1 < pieces))
        def _():
            pass_first(g + 1)
            pass_second(g + 1)

        return carry

    lax.fori_loop(0, pieces + 2, body, 0)

    rows_out[...] = rows_f[:width, :] - STEP * row_grad[:width, :]
    cols_out[...] = cols_f[:width, :]

    def sent_off(g, carry):
        def wait(kind):
            pltpu.make_async_copy(sent.at[g], sent.at[g], send_sem.at[kind, g]).wait()

        for kind in (TO_PARTNER, TO_CORE, TO_CORE_FAR, PART_A, PART_B):
            wait(kind)

        @pl.when((g < cuts) | inner)
        def _():
            wait(TO_NEAR)
            wait(TOTAL)

        @pl.when((g >= cuts) & inner)
        def _():
            wait(TO_NEAR_FAR)
            wait(TOTAL_FAR)

        @pl.when((g < cuts) | outer)
        def _():
            wait(SUM_NEAR)

        @pl.when((g >= cuts) & outer)
        def _():
            wait(SUM_NEAR_FAR)

        return carry

    lax.fori_loop(0, pieces, sent_off, 0)


def solution(mesh):
    n_blk = mesh.shape["blk"]

    def per_device(row_embed, col_embed, counts, log_marginal):
        local, width = row_embed.shape
        rounds = counts.shape[0]
        padded = -(-width // 16) * 16
        piece = local // CUTS
        pieces = rounds * CUTS
        vmem = pltpu.VMEM
        f32, half = jnp.float32, jnp.bfloat16
        block = (padded, piece)
        rows_t, cols_t = pl.pallas_call(
            functools.partial(kernel, n_blk, rounds, CUTS, piece),
            out_shape=[jax.ShapeDtypeStruct((width, local), f32)] * 2,
            in_specs=[
                pl.BlockSpec(memory_space=vmem),
                pl.BlockSpec(memory_space=vmem),
                pl.BlockSpec(memory_space=pl.ANY),
                pl.BlockSpec(memory_space=vmem),
            ],
            out_specs=[pl.BlockSpec(memory_space=vmem)] * 2,
            scratch_shapes=[
                vmem((rounds * PARTS, local, local), jnp.int32),
                vmem((pieces * PARTS, local, piece), f32),
                vmem((pieces * PARTS, local, piece), f32),
                vmem((padded, local), f32),
                vmem((padded, local), half),
                vmem((local, padded), half),
                vmem((padded, local), f32),
                vmem((padded, local), f32),
                vmem((local, 128), f32),
                vmem((pieces,) + block, half),
                vmem((PARTS, pieces) + block, half),
                vmem((2, pieces) + block, f32),
                vmem((2, pieces) + block, half),
                vmem((2, pieces) + block, half),
                vmem((2, pieces) + block, half),
                vmem((2, pieces) + block, half),
                vmem((2, pieces) + block, half),
                vmem((pieces,) + block, half),
                pltpu.SemaphoreType.DMA((rounds * PARTS,)),
                pltpu.SemaphoreType.DMA((KINDS, pieces)),
                pltpu.SemaphoreType.DMA((PARTS, pieces)),
                pltpu.SemaphoreType.DMA((2, pieces)),
                pltpu.SemaphoreType.DMA((2, pieces)),
                pltpu.SemaphoreType.DMA((pieces,)),
            ],
            compiler_params=pltpu.CompilerParams(
                collective_id=0, has_side_effects=True, vmem_limit_bytes=60 * 2**20
            ),
        )(row_embed.T, col_embed.T, counts, log_marginal.reshape(-1, 128))
        return rows_t.T, cols_t.T

    placed = (P(("blk", "rep"), None), P(("blk", "rep"), None), P(None, ("blk", "rep"), None), P())
    return jax.shard_map(
        per_device,
        mesh=mesh,
        in_specs=placed,
        out_specs=(P(("blk", "rep"), None), P(("blk", "rep"), None)),
        check_vma=False,
    )
```

```python
import functools

import jax
import jax.numpy as jnp
from jax import lax
from jax.experimental import pallas as pl
from jax.experimental.pallas import tpu as pltpu
from jax.sharding import PartitionSpec as P

STEP = 0.05
PARTS = 4
CUTS = 4
MESH = pl.DeviceIdType.MESH
TO_PARTNER, TO_CORE, TO_NEAR, TO_CORE_FAR, PART_A, PART_B, SUM_NEAR, SUM_NEAR_FAR, TOTAL, TOTAL_FAR, TO_NEAR_FAR = range(11)
KINDS = 11


def other(bit):
    return 1 - bit


def kernel(
    n_blk, rounds, cuts, piece,
    rows_ref, cols_ref, counts_ref, margin_hbm, rows_out, cols_out,
    counts, gain, shift, rows_f, rows_t, rows_n, row_grad, cols_f, row_margin,
    sent, came, part_own, part_out, part_in, near_out, near_in, total_out, total_in,
    margin_ref, rows_in, cols_in, load_sem, count_sem, send_sem, came_sem, part_sem, near_sem, total_sem,
):
    width, local = rows_ref.shape
    padded = rows_f.shape[0]
    pieces = rounds * cuts
    units = 2 * cuts
    blk = lax.axis_index("blk")
    rep = lax.axis_index("rep")
    near = rep // 2
    core = rep % 2
    far_rep = other(near) * 2 + core
    inner = (blk + near) % 2 == 1
    outer = (blk + near) % 2 == 0
    across = (blk + n_blk // 2) % n_blk
    along = blk + 1 - 2 * (blk % 2)
    both = across + 1 - 2 * (across % 2)
    core_id = (blk, near * 2 + other(core))
    near_id = (blk, far_rep)
    across_id = (across, rep)
    along_id = (along, rep)
    touch_id = (along, far_rep)
    both_along_id = (both, rep)
    both_touch_id = (both, far_rep)
    partners = (core_id, near_id, across_id, along_id)

    barrier = pltpu.get_barrier_semaphore()
    for partner in partners:
        pl.semaphore_signal(barrier, inc=1, device_id=partner, device_id_type=MESH)

    def part_of(d):
        return ((near + d // 2) % 2) * 2 + (core + d % 2) % 2

    def count_copy(rnd, d):
        start = pl.multiple_of(part_of(d) * local, local)
        return pltpu.make_async_copy(
            counts_ref.at[rnd, :, pl.ds(start, local)], counts.at[rnd * PARTS + d], count_sem.at[rnd * PARTS + d]
        )

    loads = [
        pltpu.make_async_copy(cols_ref, cols_in, load_sem.at[0]),
        pltpu.make_async_copy(rows_ref, rows_in, load_sem.at[1]),
        pltpu.make_async_copy(margin_hbm, margin_ref, load_sem.at[2]),
    ]
    for load in loads:
        load.start()
    for rnd in range(rounds):
        for d in range(PARTS):
            count_copy(rnd, d).start()

    def send(kind, g, src, dst, sem, target):
        pltpu.make_async_remote_copy(
            src_ref=src, dst_ref=dst, send_sem=send_sem.at[kind, g], recv_sem=sem, device_id=target, device_id_type=MESH
        ).start()

    def landed(ref, sem):
        pltpu.make_async_copy(ref, ref, sem).wait()

    def lanes(j):
        return pl.ds(pl.multiple_of(j * piece, piece), piece)

    cols_f[width:, :] = jnp.zeros((padded - width, local), jnp.float32)
    rows_f[width:, :] = jnp.zeros((padded - width, local), jnp.float32)
    loads[0].wait()
    cols_f[:width, :] = cols_in[...]
    for j in range(cuts):
        sent[j] = cols_f[:, j * piece : (j + 1) * piece].astype(jnp.bfloat16)
    pl.semaphore_wait(barrier, len(partners))
    for j in range(cuts):
        send(TO_PARTNER, j, sent.at[j], came.at[0, j], came_sem.at[0, j], across_id)

    loads[1].wait()
    rows_f[:width, :] = rows_in[...]

    def set_rows():
        rows = rows_f[...]
        rows_t[...] = rows.astype(jnp.bfloat16)
        rows_n[...] = rows.T.astype(jnp.bfloat16)
        row_grad[...] = jnp.zeros_like(row_grad)

    set_rows()
    loads[2].wait()
    margins = margin_ref[...]
    most = jnp.max(jnp.max(margins, axis=0, keepdims=True), axis=1, keepdims=True)
    mass = jnp.sum(jnp.sum(jnp.exp(margins - most), axis=0, keepdims=True), axis=1, keepdims=True)
    log_total = jnp.log(mass) + most
    lines = local // 128
    for k in range(lines):
        line = margin_ref[pl.ds((blk * PARTS + rep) * lines + k, 1), :]
        row_margin[k * 128 : (k + 1) * 128, :] = jnp.broadcast_to(line, (128, 128)).T - log_total

    scale = float(1.0 / (PARTS * local) ** 0.5)

    def prepare(g, k):
        rnd, j = g // cuts, g % cuts
        partner = across + rnd * (along - across)

        @pl.when(j == 0)
        def _():
            for h in range(2):
                count_copy(rnd, 2 * k + h).wait()

        for h in range(2):
            d = 2 * k + h
            first = (partner * PARTS + part_of(d)) * lines + j
            number = counts[rnd * PARTS + d, :, lanes(j)]
            count = number.astype(jnp.float32)
            least = jnp.maximum(count, 1.0)
            confidence = scale * 0.1 + (scale * 0.25) * (count * lax.rsqrt(least))
            gain[g * 2 + k, :, h * piece : (h + 1) * piece] = jnp.where(number > 0, confidence, -0.5)
            shift[g * 2 + k, :, h * piece : (h + 1) * piece] = (
                row_margin[...] + margin_ref[pl.ds(first, 1), :]
            ) - jnp.log(least)

    def compute(g, k):
        block = jnp.concatenate([came[2 * k, g], came[2 * k + 1, g]], axis=1)
        pred = jnp.dot(rows_n[...], block, preferred_element_type=jnp.float32)
        factor = gain[g * 2 + k]
        value = factor * (pred + shift[g * 2 + k])
        smooth = (0.5 * scale) - (0.5 * scale) * jnp.tanh(value)
        slope = jnp.where(factor > 0.0, value, smooth).astype(jnp.bfloat16)
        far = jnp.dot(rows_t[...], slope, preferred_element_type=jnp.float32)
        part_own[k, g] = far[:, :piece]
        part_out[k, g] = far[:, piece:]
        send(PART_A + k, g, part_out.at[k, g], part_in.at[k, g], part_sem.at[k, g], core_id)
        row_grad[...] += lax.dot_general(block, slope, (((1,), (1,)), ((), ())), preferred_element_type=jnp.float32)

    def arrived(d, g):
        landed(came.at[d, g], came_sem.at[d, g])

    def pass_first(g):
        arrived(0, g)
        send(TO_CORE, g, came.at[0, g], came.at[1, g], came_sem.at[1, g], core_id)

        def on():
            send(TO_NEAR, g, came.at[0, g], came.at[2, g], came_sem.at[2, g], near_id)

        on() if g < cuts else pl.when(inner)(on)

    def pass_second(g):
        arrived(2, g)
        send(TO_CORE_FAR, g, came.at[2, g], came.at[3, g], came_sem.at[3, g], core_id)
        if g >= cuts:
            @pl.when(inner)
            def _():
                send(TO_NEAR_FAR, g, came.at[2, g], came.at[0, g], came_sem.at[0, g], near_id)

    def chip_sum(g, k):
        landed(part_in.at[k, g], part_sem.at[k, g])
        return part_own[k, g] + part_in[k, g]

    def to_near(g, k):
        near_out[1 - k, g] = chip_sum(g, k).astype(jnp.bfloat16)
        send(SUM_NEAR + 1 - k, g, near_out.at[1 - k, g], near_in.at[1 - k, g], near_sem.at[1 - k, g], near_id)

    def both_sum(g, k):
        own = chip_sum(g, k)
        landed(near_in.at[k, g], near_sem.at[k, g])
        return own + near_in[k, g].astype(jnp.float32)

    def total_first(g):
        later = g + cuts
        total = both_sum(g, 0)
        sent[later] = (came[0, g].astype(jnp.float32) - STEP * total).astype(jnp.bfloat16)

        @pl.when(outer)
        def _():
            send(TO_PARTNER, later, sent.at[later], came.at[0, later], came_sem.at[0, later], both_along_id)

        @pl.when(inner)
        def _():
            send(TO_PARTNER, later, sent.at[later], came.at[2, later], came_sem.at[2, later], both_touch_id)

        total_out[0, g] = total.astype(jnp.bfloat16)
        send(TOTAL, g, total_out.at[0, g], total_in.at[g], total_sem.at[g], across_id)

    def total_last(g):
        total_out[0, g] = both_sum(g, 0).astype(jnp.bfloat16)
        send(TOTAL, g, total_out.at[0, g], total_in.at[g], total_sem.at[g], along_id)
        total_out[1, g] = both_sum(g, 1).astype(jnp.bfloat16)
        send(TOTAL_FAR, g, total_out.at[1, g], total_in.at[g], total_sem.at[g], touch_id)

    def finish(g):
        j = g % cuts
        landed(total_in.at[g], total_sem.at[g])
        spot = slice(j * piece, (j + 1) * piece)
        cols_f[:, spot] = cols_f[:, spot] - STEP * total_in[g].astype(jnp.float32)

    def new_rows():
        rows_f[...] = rows_f[...] - STEP * row_grad[...]
        set_rows()

    def ready(s, carry):
        prepare(s // 2, s % 2)
        return carry

    lax.fori_loop(0, units, ready, 0)

    def ready_more(low, high):
        lax.fori_loop(units + low, units + high, ready, 0)

    ahead = [
        [(pass_first, 0), (arrived, 1, 0)],
        [(pass_first, 1), (arrived, 1, 1)],
        [(pass_first, 2), (pass_second, 0), (arrived, 3, 0)],
        [(arrived, 1, 2)],
        [(pass_first, 3), (pass_second, 1), (arrived, 3, 1)],
        [(arrived, 1, 3)],
        [(to_near, 0, 1), (pass_second, 2), (arrived, 3, 2)],
        [(to_near, 1, 1), (pass_second, 3), (arrived, 3, 3)],
        [
            (to_near, 2, 1), (total_first, 0), (to_near, 3, 1), (new_rows,), (total_first, 1), (ready_more, 0, 3),
            (total_first, 2), (ready_more, 3, 6), (total_first, 3), (ready_more, 6, 8), (pass_first, 4), (pass_second, 4),
            (arrived, 1, 4),
        ],
        [(arrived, 3, 4)],
    ]
    for g in range(cuts + 1, pieces):
        ahead.append(["outer", (to_near, g - 1, 0), (to_near, g - 1, 1), "all", (pass_first, g), (pass_second, g), (arrived, 1, g)])
        if g == cuts + 2:
            ahead[-1] += [(finish, 0), (finish, 1)]
        if g == cuts + 3:
            ahead[-1] += [(finish, 2), (finish, 3)]
        ahead.append([(arrived, 3, g)])

    def act(steps):
        mine, rest = [], []
        for step in steps:
            if step == "outer":
                rest = mine
                mine = []
            elif step == "all":
                todo = mine

                @pl.when(outer)
                def _():
                    for call, *args in todo:
                        call(*args)

                mine = []
            else:
                mine.append(step)
        for call, *args in mine:
            call(*args)

    def body(t, carry):
        rnd, s = t // units, t % units
        k0 = other(s % 2) * ((s + units - 1) // units) + s // (units - 1)
        j0 = (s + 1) // 2 - k0
        j = j0 + rnd * (s // 2 - j0)
        k = k0 + rnd * (s % 2 - k0)
        g = rnd * cuts + j

        for start in range(0, len(ahead), 4):
            @pl.when((t >= start) & (t < start + 4))
            def _():
                for now in range(start, start + 4):
                    pl.when(t == now)(functools.partial(act, ahead[now]))

        compute(g, k)
        return carry

    lax.fori_loop(0, rounds * units, body, 0)

    @pl.when(outer)
    def _():
        to_near(pieces - 1, 0)
        to_near(pieces - 1, 1)

    rows_out[...] = rows_f[:width, :] - STEP * row_grad[:width, :]

    @pl.when(inner)
    def _():
        for g in range(cuts, pieces):
            total_last(g)

    for g in range(cuts, pieces):
        finish(g)
    cols_out[...] = cols_f[:width, :]

    def sent_off(g, carry):
        def wait(kind, ref):
            pltpu.make_async_copy(ref, ref, send_sem.at[kind, g]).wait()

        for kind in (TO_PARTNER, TO_CORE, TO_CORE_FAR):
            wait(kind, sent.at[g])
        for kind in (PART_A, PART_B):
            wait(kind, part_out.at[0, g])

        @pl.when((g < cuts) | inner)
        def _():
            wait(TO_NEAR, sent.at[g])
            wait(TOTAL, sent.at[g])

        @pl.when((g >= cuts) & inner)
        def _():
            wait(TO_NEAR_FAR, sent.at[g])
            wait(TOTAL_FAR, sent.at[g])

        @pl.when((g < cuts) | outer)
        def _():
            wait(SUM_NEAR, sent.at[g])

        @pl.when((g >= cuts) & outer)
        def _():
            wait(SUM_NEAR_FAR, sent.at[g])

        return carry

    lax.fori_loop(0, pieces, sent_off, 0)


def settle(rows_ref, cols_ref, rows_out, cols_out, sem):
    copies = [
        pltpu.make_async_copy(rows_ref, rows_out, sem.at[0]),
        pltpu.make_async_copy(cols_ref, cols_out, sem.at[1]),
    ]
    for copy in copies:
        copy.start()
    for copy in copies:
        copy.wait()


def solution(mesh):
    n_blk = mesh.shape["blk"]

    def per_device(row_embed, col_embed, counts, log_marginal):
        local, width = row_embed.shape
        rounds = counts.shape[0]
        padded = -(-width // 16) * 16
        piece = local // CUTS
        pieces = rounds * CUTS
        vmem = pltpu.VMEM
        f32, half = jnp.float32, jnp.bfloat16
        block = (padded, piece)
        rows_t, cols_t = pl.pallas_call(
            functools.partial(kernel, n_blk, rounds, CUTS, piece),
            out_shape=[jax.ShapeDtypeStruct((width, local), f32)] * 2,
            in_specs=[
                pl.BlockSpec(memory_space=pl.ANY),
                pl.BlockSpec(memory_space=pl.ANY),
                pl.BlockSpec(memory_space=pl.ANY),
                pl.BlockSpec(memory_space=pl.ANY),
            ],
            out_specs=[pl.BlockSpec(memory_space=vmem)] * 2,
            scratch_shapes=[
                vmem((rounds * PARTS, local, local), jnp.int32),
                vmem((pieces * 2, local, 2 * piece), f32),
                vmem((pieces * 2, local, 2 * piece), f32),
                vmem((padded, local), f32),
                vmem((padded, local), half),
                vmem((local, padded), half),
                vmem((padded, local), f32),
                vmem((padded, local), f32),
                vmem((local, 128), f32),
                vmem((pieces,) + block, half),
                vmem((PARTS, pieces) + block, half),
                vmem((2, pieces) + block, f32),
                vmem((2, pieces) + block, f32),
                vmem((2, pieces) + block, f32),
                vmem((2, pieces) + block, half),
                vmem((2, pieces) + block, half),
                vmem((2, pieces) + block, half),
                vmem((pieces,) + block, half),
                vmem((local * PARTS * n_blk // 128, 128), f32),
                vmem((width, local), f32),
                vmem((width, local), f32),
                pltpu.SemaphoreType.DMA((3,)),
                pltpu.SemaphoreType.DMA((rounds * PARTS,)),
                pltpu.SemaphoreType.DMA((KINDS, pieces)),
                pltpu.SemaphoreType.DMA((PARTS, pieces)),
                pltpu.SemaphoreType.DMA((2, pieces)),
                pltpu.SemaphoreType.DMA((2, pieces)),
                pltpu.SemaphoreType.DMA((pieces,)),
            ],
            compiler_params=pltpu.CompilerParams(
                collective_id=0, has_side_effects=True, vmem_limit_bytes=52 * 2**20
            ),
        )(row_embed.T, col_embed.T, counts, log_marginal.reshape(-1, 128))
        rows_t, cols_t = pl.pallas_call(
            settle,
            out_shape=[jax.ShapeDtypeStruct((width, local), f32)] * 2,
            in_specs=[pl.BlockSpec(memory_space=pl.ANY)] * 2,
            out_specs=[pl.BlockSpec(memory_space=pl.ANY)] * 2,
            scratch_shapes=[pltpu.SemaphoreType.DMA((2,))],
            compiler_params=pltpu.CompilerParams(vmem_limit_bytes=2**20),
        )(rows_t, cols_t)
        return rows_t.T, cols_t.T

    placed = (P(("blk", "rep"), None), P(("blk", "rep"), None), P(None, ("blk", "rep"), None), P())
    return jax.shard_map(
        per_device,
        mesh=mesh,
        in_specs=placed,
        out_specs=(P(("blk", "rep"), None), P(("blk", "rep"), None)),
        check_vma=False,
    )
```

```python
import functools

import jax
import jax.numpy as jnp
from jax import lax
from jax.experimental import pallas as pl
from jax.experimental.pallas import tpu as pltpu
from jax.sharding import PartitionSpec as P

STEP = 0.05
PARTS = 4
CUTS = 4
MESH = pl.DeviceIdType.MESH
TO_PARTNER, TO_CORE, TO_NEAR, TO_CORE_FAR, PART_A, PART_B, SUM_NEAR, SUM_NEAR_FAR, TOTAL, TOTAL_FAR, TO_NEAR_FAR = range(11)
KINDS = 11


def other(bit):
    return 1 - bit


def kernel(
    n_blk, rounds, cuts, piece,
    rows_ref, cols_ref, counts_ref, margin_hbm, rows_out, cols_out,
    counts, gain, shift, rows_f, rows_t, rows_n, row_grad, cols_f, row_margin,
    sent, came, part_own, part_out, part_in, near_out, near_in, total_out, total_in,
    margin_ref, rows_in, cols_in, load_sem, count_sem, send_sem, came_sem, part_sem, near_sem, total_sem,
):
    width, local = rows_ref.shape
    padded = rows_f.shape[0]
    pieces = rounds * cuts
    units = 2 * cuts
    blk = lax.axis_index("blk")
    rep = lax.axis_index("rep")
    near = rep // 2
    core = rep % 2
    far_rep = other(near) * 2 + core
    inner = (blk + near) % 2 == 1
    outer = (blk + near) % 2 == 0
    across = (blk + n_blk // 2) % n_blk
    along = blk + 1 - 2 * (blk % 2)
    both = across + 1 - 2 * (across % 2)
    core_id = (blk, near * 2 + other(core))
    near_id = (blk, far_rep)
    across_id = (across, rep)
    along_id = (along, rep)
    touch_id = (along, far_rep)
    both_along_id = (both, rep)
    both_touch_id = (both, far_rep)
    partners = (core_id, near_id, across_id, along_id)

    barrier = pltpu.get_barrier_semaphore()
    for partner in partners:
        pl.semaphore_signal(barrier, inc=1, device_id=partner, device_id_type=MESH)

    def part_of(d):
        return ((near + d // 2) % 2) * 2 + (core + d % 2) % 2

    def count_copy(rnd, d):
        start = pl.multiple_of(part_of(d) * local, local)
        return pltpu.make_async_copy(
            counts_ref.at[rnd, :, pl.ds(start, local)], counts.at[rnd * PARTS + d], count_sem.at[rnd * PARTS + d]
        )

    loads = [
        pltpu.make_async_copy(cols_ref, cols_in, load_sem.at[0]),
        pltpu.make_async_copy(rows_ref, rows_in, load_sem.at[1]),
        pltpu.make_async_copy(margin_hbm, margin_ref, load_sem.at[2]),
    ]
    for load in loads:
        load.start()
    for rnd in range(rounds):
        for d in range(PARTS):
            count_copy(rnd, d).start()

    def send(kind, g, src, dst, sem, target):
        pltpu.make_async_remote_copy(
            src_ref=src, dst_ref=dst, send_sem=send_sem.at[kind], recv_sem=sem, device_id=target, device_id_type=MESH
        ).start()

    def landed(ref, sem):
        pltpu.make_async_copy(ref, ref, sem).wait()

    def lanes(j):
        return pl.ds(pl.multiple_of(j * piece, piece), piece)

    cols_f[width:, :] = jnp.zeros((padded - width, local), jnp.float32)
    rows_f[width:, :] = jnp.zeros((padded - width, local), jnp.float32)
    loads[0].wait()
    cols_f[:width, :] = cols_in[...]
    for j in range(cuts):
        sent[j] = cols_f[:, j * piece : (j + 1) * piece].astype(jnp.bfloat16)
    pl.semaphore_wait(barrier, len(partners))
    for j in range(cuts):
        send(TO_PARTNER, j, sent.at[j], came.at[0, j], came_sem.at[0, j], across_id)

    loads[1].wait()
    rows_f[:width, :] = rows_in[...]

    def set_rows():
        rows = rows_f[...]
        rows_t[...] = rows.astype(jnp.bfloat16)
        rows_n[...] = rows.T.astype(jnp.bfloat16)
        row_grad[...] = jnp.zeros_like(row_grad)

    set_rows()
    loads[2].wait()
    margins = margin_ref[...]
    most = jnp.max(jnp.max(margins, axis=0, keepdims=True), axis=1, keepdims=True)
    mass = jnp.sum(jnp.sum(jnp.exp(margins - most), axis=0, keepdims=True), axis=1, keepdims=True)
    log_total = jnp.log(mass) + most
    lines = local // 128
    for k in range(lines):
        line = margin_ref[pl.ds((blk * PARTS + rep) * lines + k, 1), :]
        row_margin[k * 128 : (k + 1) * 128, :] = jnp.broadcast_to(line, (128, 128)).T - log_total

    scale = float(1.0 / (PARTS * local) ** 0.5)

    def prepare(g, k):
        rnd, j = g // cuts, g % cuts
        partner = across + rnd * (along - across)

        @pl.when(j == 0)
        def _():
            for h in range(2):
                count_copy(rnd, 2 * k + h).wait()

        for h in range(2):
            d = 2 * k + h
            first = (partner * PARTS + part_of(d)) * lines + j
            number = counts[rnd * PARTS + d, :, lanes(j)]
            count = number.astype(jnp.float32)
            least = jnp.maximum(count, 1.0)
            confidence = scale * 0.1 + (scale * 0.25) * (count * lax.rsqrt(least))
            gain[g * 2 + k, :, h * piece : (h + 1) * piece] = jnp.where(number > 0, confidence, -0.5)
            shift[g * 2 + k, :, h * piece : (h + 1) * piece] = (
                row_margin[...] + margin_ref[pl.ds(first, 1), :]
            ) - jnp.log(least)

    def compute(g, k):
        block = jnp.concatenate([came[2 * k, g], came[2 * k + 1, g]], axis=1)
        slopes = []
        height = local // 4
        for part in range(4):
            span = slice(part * height, (part + 1) * height)
            pred = jnp.dot(rows_n[span, :], block, preferred_element_type=jnp.float32)
            factor = gain[g * 2 + k, span, :]
            value = factor * (pred + shift[g * 2 + k, span, :])
            smooth = (0.5 * scale) - (0.5 * scale) * jnp.tanh(value)
            slopes.append(jnp.where(factor > 0.0, value, smooth).astype(jnp.bfloat16))
        slope = jnp.concatenate(slopes, axis=0)
        far = jnp.dot(rows_t[...], slope, preferred_element_type=jnp.float32)
        part_own[k, g] = far[:, :piece]
        part_out[k, g] = far[:, piece:]
        send(PART_A + k, g, part_out.at[k, g], part_in.at[k, g], part_sem.at[k, g], core_id)
        row_grad[...] += lax.dot_general(block, slope, (((1,), (1,)), ((), ())), preferred_element_type=jnp.float32)

    def arrived(d, g):
        landed(came.at[d, g], came_sem.at[d, g])

    def pass_first(g):
        arrived(0, g)
        send(TO_CORE, g, came.at[0, g], came.at[1, g], came_sem.at[1, g], core_id)

        def on():
            send(TO_NEAR, g, came.at[0, g], came.at[2, g], came_sem.at[2, g], near_id)

        on() if g < cuts else pl.when(inner)(on)

    def pass_second(g):
        arrived(2, g)
        send(TO_CORE_FAR, g, came.at[2, g], came.at[3, g], came_sem.at[3, g], core_id)
        if g >= cuts:
            @pl.when(inner)
            def _():
                send(TO_NEAR_FAR, g, came.at[2, g], came.at[0, g], came_sem.at[0, g], near_id)

    def chip_sum(g, k):
        landed(part_in.at[k, g], part_sem.at[k, g])
        return part_own[k, g] + part_in[k, g]

    def to_near(g, k):
        near_out[1 - k, g] = chip_sum(g, k).astype(jnp.bfloat16)
        send(SUM_NEAR + 1 - k, g, near_out.at[1 - k, g], near_in.at[1 - k, g], near_sem.at[1 - k, g], near_id)

    def both_sum(g, k):
        own = chip_sum(g, k)
        landed(near_in.at[k, g], near_sem.at[k, g])
        return own + near_in[k, g].astype(jnp.float32)

    def total_first(g):
        later = g + cuts
        total = both_sum(g, 0)
        sent[later] = (came[0, g].astype(jnp.float32) - STEP * total).astype(jnp.bfloat16)

        @pl.when(outer)
        def _():
            send(TO_PARTNER, later, sent.at[later], came.at[0, later], came_sem.at[0, later], both_along_id)

        @pl.when(inner)
        def _():
            send(TO_PARTNER, later, sent.at[later], came.at[2, later], came_sem.at[2, later], both_touch_id)

        total_out[0, g] = total.astype(jnp.bfloat16)
        send(TOTAL, g, total_out.at[0, g], total_in.at[g], total_sem.at[g], across_id)

    def total_last(g):
        total_out[0, g] = both_sum(g, 0).astype(jnp.bfloat16)
        send(TOTAL, g, total_out.at[0, g], total_in.at[g], total_sem.at[g], along_id)
        total_out[1, g] = both_sum(g, 1).astype(jnp.bfloat16)
        send(TOTAL_FAR, g, total_out.at[1, g], total_in.at[g], total_sem.at[g], touch_id)

    def finish(g):
        j = g % cuts
        landed(total_in.at[g], total_sem.at[g])
        spot = slice(j * piece, (j + 1) * piece)
        new = cols_f[:, spot] - STEP * total_in[g].astype(jnp.float32)
        if g < pieces - cuts:
            cols_f[:, spot] = new
        else:
            cols_out[:, spot] = new[:width, :]

    def new_rows():
        rows_f[...] = rows_f[...] - STEP * row_grad[...]
        set_rows()

    def ready(s, carry):
        prepare(s // 2, s % 2)
        return carry

    lax.fori_loop(0, units, ready, 0)

    def ready_more(low, high):
        lax.fori_loop(units + low, units + high, ready, 0)

    ahead = [
        [(pass_first, 0), (arrived, 1, 0)],
        [(pass_first, 1), (arrived, 1, 1)],
        [(pass_first, 2), (pass_second, 0), (arrived, 3, 0)],
        [(arrived, 1, 2)],
        [(pass_first, 3), (pass_second, 1), (arrived, 3, 1)],
        [(arrived, 1, 3)],
        [(to_near, 0, 1), (pass_second, 2), (arrived, 3, 2)],
        [(to_near, 1, 1), (total_first, 0), (pass_second, 3), (arrived, 3, 3)],
        [
            (to_near, 2, 1), (to_near, 3, 1), (new_rows,), (total_first, 1), (ready_more, 0, 3),
            (total_first, 2), (ready_more, 3, 6), (total_first, 3), (ready_more, 6, 8), (pass_first, 4), (pass_second, 4),
            (arrived, 1, 4),
        ],
        [(arrived, 3, 4)],
    ]
    for g in range(cuts + 1, pieces):
        ahead.append(["outer", (to_near, g - 1, 1), (to_near, g - 1, 0), "all", (pass_first, g), (pass_second, g), (arrived, 1, g)])
        if g == cuts + 2:
            ahead[-1] += [(finish, 0), (finish, 1)]
        if g == cuts + 3:
            ahead[-1] += [(finish, 2), (finish, 3)]
        ahead.append([(arrived, 3, g)])

    def act(steps):
        mine, rest = [], []
        for step in steps:
            if step == "outer":
                rest = mine
                mine = []
            elif step == "all":
                todo = mine

                @pl.when(outer)
                def _():
                    for call, *args in todo:
                        call(*args)

                mine = []
            else:
                mine.append(step)
        for call, *args in mine:
            call(*args)

    def body(t, carry):
        rnd, s = t // units, t % units
        k0 = other(s % 2) * ((s + units - 1) // units) + s // (units - 1)
        j0 = (s + 1) // 2 - k0
        j = j0 + rnd * (s // 2 - j0)
        k = k0 + rnd * (s % 2 - k0)
        g = rnd * cuts + j

        for start in range(0, len(ahead), 4):
            @pl.when((t >= start) & (t < start + 4))
            def _():
                for now in range(start, start + 4):
                    pl.when(t == now)(functools.partial(act, ahead[now]))

        compute(g, k)
        return carry

    lax.fori_loop(0, rounds * units, body, 0)

    @pl.when(outer)
    def _():
        to_near(pieces - 1, 1)
        to_near(pieces - 1, 0)

    rows_out[...] = rows_f[:width, :] - STEP * row_grad[:width, :]

    @pl.when(inner)
    def _():
        for g in range(cuts, pieces):
            total_last(g)

    for g in range(cuts, pieces):
        finish(g)

    def sent_off(kind, ref):
        pltpu.make_async_copy(ref, ref, send_sem.at[kind]).wait()

    half = sent.at[:cuts]
    for kind in (TO_PARTNER, TO_CORE, TO_CORE_FAR):
        sent_off(kind, sent)
    for kind in (PART_A, PART_B):
        sent_off(kind, part_out.at[0])

    @pl.when(inner)
    def _():
        for kind, ref in ((TO_NEAR, sent), (TOTAL, sent), (TO_NEAR_FAR, half), (TOTAL_FAR, half), (SUM_NEAR, half)):
            sent_off(kind, ref)

    @pl.when(outer)
    def _():
        for kind, ref in ((TO_NEAR, half), (TOTAL, half), (SUM_NEAR, sent), (SUM_NEAR_FAR, half)):
            sent_off(kind, ref)


def settle(rows_ref, cols_ref, rows_out, cols_out, sem):
    copies = [
        pltpu.make_async_copy(rows_ref, rows_out, sem.at[0]),
        pltpu.make_async_copy(cols_ref, cols_out, sem.at[1]),
    ]
    for copy in copies:
        copy.start()
    for copy in copies:
        copy.wait()


def solution(mesh):
    n_blk = mesh.shape["blk"]

    def per_device(row_embed, col_embed, counts, log_marginal):
        local, width = row_embed.shape
        rounds = counts.shape[0]
        padded = -(-width // 16) * 16
        piece = local // CUTS
        pieces = rounds * CUTS
        vmem = pltpu.VMEM
        f32, half = jnp.float32, jnp.bfloat16
        block = (padded, piece)
        rows_t, cols_t = pl.pallas_call(
            functools.partial(kernel, n_blk, rounds, CUTS, piece),
            out_shape=[jax.ShapeDtypeStruct((width, local), f32)] * 2,
            in_specs=[
                pl.BlockSpec(memory_space=pl.ANY),
                pl.BlockSpec(memory_space=pl.ANY),
                pl.BlockSpec(memory_space=pl.ANY),
                pl.BlockSpec(memory_space=pl.ANY),
            ],
            out_specs=[pl.BlockSpec(memory_space=vmem)] * 2,
            scratch_shapes=[
                vmem((rounds * PARTS, local, local), jnp.int32),
                vmem((pieces * 2, local, 2 * piece), f32),
                vmem((pieces * 2, local, 2 * piece), f32),
                vmem((padded, local), f32),
                vmem((padded, local), half),
                vmem((local, padded), half),
                vmem((padded, local), f32),
                vmem((padded, local), f32),
                vmem((local, 128), f32),
                vmem((pieces,) + block, half),
                vmem((PARTS, pieces) + block, half),
                vmem((2, pieces) + block, f32),
                vmem((2, pieces) + block, f32),
                vmem((2, pieces) + block, f32),
                vmem((2, pieces) + block, half),
                vmem((2, pieces) + block, half),
                vmem((2, pieces) + block, half),
                vmem((pieces,) + block, half),
                vmem((local * PARTS * n_blk // 128, 128), f32),
                vmem((width, local), f32),
                vmem((width, local), f32),
                pltpu.SemaphoreType.DMA((3,)),
                pltpu.SemaphoreType.DMA((rounds * PARTS,)),
                pltpu.SemaphoreType.DMA((KINDS,)),
                pltpu.SemaphoreType.DMA((PARTS, pieces)),
                pltpu.SemaphoreType.DMA((2, pieces)),
                pltpu.SemaphoreType.DMA((2, pieces)),
                pltpu.SemaphoreType.DMA((pieces,)),
            ],
            compiler_params=pltpu.CompilerParams(
                collective_id=0, has_side_effects=True, vmem_limit_bytes=52 * 2**20
            ),
        )(row_embed.T, col_embed.T, counts, log_marginal.reshape(-1, 128))
        rows_t, cols_t = pl.pallas_call(
            settle,
            out_shape=[jax.ShapeDtypeStruct((width, local), f32)] * 2,
            in_specs=[pl.BlockSpec(memory_space=pl.ANY)] * 2,
            out_specs=[pl.BlockSpec(memory_space=pl.ANY)] * 2,
            scratch_shapes=[pltpu.SemaphoreType.DMA((2,))],
            compiler_params=pltpu.CompilerParams(vmem_limit_bytes=2**20),
        )(rows_t, cols_t)
        return rows_t.T, cols_t.T

    placed = (P(("blk", "rep"), None), P(("blk", "rep"), None), P(None, ("blk", "rep"), None), P())
    return jax.shard_map(
        per_device,
        mesh=mesh,
        in_specs=placed,
        out_specs=(P(("blk", "rep"), None), P(("blk", "rep"), None)),
        check_vma=False,
    )
```

```python
import functools

import jax
import jax.numpy as jnp
from jax import lax
from jax.experimental import pallas as pl
from jax.experimental.pallas import tpu as pltpu
from jax.sharding import PartitionSpec as P

STEP = 0.05
PARTS = 4
CUTS = 4
MESH = pl.DeviceIdType.MESH
TO_PARTNER, TO_CORE, TO_NEAR, TO_CORE_FAR, PART_A, PART_B, SUM_NEAR, SUM_NEAR_FAR, TOTAL, TOTAL_FAR, TO_NEAR_FAR = range(11)
KINDS = 11


def other(bit):
    return 1 - bit


def kernel(
    n_blk, rounds, cuts, piece,
    rows_ref, cols_ref, counts_ref, margin_hbm, rows_out, cols_out,
    counts, gain, shift, rows_f, rows_t, rows_n, row_grad, cols_f, row_margin,
    sent, came, part_own, part_out, part_in, near_out, near_in, total_out, total_in,
    margin_ref, rows_in, cols_in, load_sem, count_sem, send_sem, came_sem, part_sem, near_sem, total_sem,
):
    width, local = rows_ref.shape
    padded = rows_f.shape[0]
    pieces = rounds * cuts
    units = 2 * cuts
    blk = lax.axis_index("blk")
    rep = lax.axis_index("rep")
    near = rep // 2
    core = rep % 2
    far_rep = other(near) * 2 + core
    inner = (blk + near) % 2 == 1
    outer = (blk + near) % 2 == 0
    across = (blk + n_blk // 2) % n_blk
    along = blk + 1 - 2 * (blk % 2)
    both = across + 1 - 2 * (across % 2)
    core_id = (blk, near * 2 + other(core))
    near_id = (blk, far_rep)
    across_id = (across, rep)
    along_id = (along, rep)
    touch_id = (along, far_rep)
    both_along_id = (both, rep)
    both_touch_id = (both, far_rep)
    partners = (core_id, near_id, across_id, along_id)

    barrier = pltpu.get_barrier_semaphore()
    for partner in partners:
        pl.semaphore_signal(barrier, inc=1, device_id=partner, device_id_type=MESH)

    def part_of(d):
        return ((near + d // 2) % 2) * 2 + (core + d % 2) % 2

    def count_copy(rnd, d):
        start = pl.multiple_of(part_of(d) * local, local)
        return pltpu.make_async_copy(
            counts_ref.at[rnd, :, pl.ds(start, local)], counts.at[rnd * PARTS + d], count_sem.at[rnd * PARTS + d]
        )

    loads = [
        pltpu.make_async_copy(cols_ref, cols_in, load_sem.at[0]),
        pltpu.make_async_copy(rows_ref, rows_in, load_sem.at[1]),
        pltpu.make_async_copy(margin_hbm, margin_ref, load_sem.at[2]),
    ]
    for load in loads:
        load.start()
    for rnd in range(rounds):
        for d in range(PARTS):
            count_copy(rnd, d).start()

    def send(kind, g, src, dst, sem, target):
        pltpu.make_async_remote_copy(
            src_ref=src, dst_ref=dst, send_sem=send_sem.at[kind], recv_sem=sem, device_id=target, device_id_type=MESH
        ).start()

    def landed(ref, sem):
        pltpu.make_async_copy(ref, ref, sem).wait()

    def lanes(j):
        return pl.ds(pl.multiple_of(j * piece, piece), piece)

    cols_f[width:, :] = jnp.zeros((padded - width, local), jnp.float32)
    rows_f[width:, :] = jnp.zeros((padded - width, local), jnp.float32)
    loads[0].wait()
    cols_f[:width, :] = cols_in[...]
    for j in range(cuts):
        sent[j] = cols_f[:, j * piece : (j + 1) * piece].astype(jnp.bfloat16)
    pl.semaphore_wait(barrier, len(partners))
    for j in range(cuts):
        send(TO_PARTNER, j, sent.at[j], came.at[0, j], came_sem.at[0, j], across_id)

    loads[1].wait()
    rows_f[:width, :] = rows_in[...]

    def set_rows():
        rows = rows_f[...]
        rows_t[...] = rows.astype(jnp.bfloat16)
        rows_n[...] = rows.T.astype(jnp.bfloat16)
        row_grad[...] = jnp.zeros_like(row_grad)

    set_rows()
    loads[2].wait()
    margins = margin_ref[...]
    most = jnp.max(jnp.max(margins, axis=0, keepdims=True), axis=1, keepdims=True)
    mass = jnp.sum(jnp.sum(jnp.exp(margins - most), axis=0, keepdims=True), axis=1, keepdims=True)
    log_total = jnp.log(mass) + most
    lines = local // 128
    for k in range(lines):
        line = margin_ref[pl.ds((blk * PARTS + rep) * lines + k, 1), :]
        row_margin[k * 128 : (k + 1) * 128, :] = jnp.broadcast_to(line, (128, 128)).T - log_total

    scale = float(1.0 / (PARTS * local) ** 0.5)

    def prepare(g, k):
        rnd, j = g // cuts, g % cuts
        partner = across + rnd * (along - across)

        @pl.when(j == 0)
        def _():
            for h in range(2):
                count_copy(rnd, 2 * k + h).wait()

        for h in range(2):
            d = 2 * k + h
            first = (partner * PARTS + part_of(d)) * lines + j
            number = counts[rnd * PARTS + d, :, lanes(j)]
            count = number.astype(jnp.float32)
            least = jnp.maximum(count, 1.0)
            confidence = scale * 0.1 + (scale * 0.25) * (count * lax.rsqrt(least))
            gain[g * 2 + k, :, h * piece : (h + 1) * piece] = jnp.where(number > 0, confidence, -0.5)
            shift[g * 2 + k, :, h * piece : (h + 1) * piece] = (
                row_margin[...] + margin_ref[pl.ds(first, 1), :]
            ) - jnp.log(least)

    def compute(g, k):
        block = jnp.concatenate([came[2 * k, g], came[2 * k + 1, g]], axis=1)
        slopes = []
        height = local // 4
        for part in range(4):
            span = slice(part * height, (part + 1) * height)
            pred = jnp.dot(rows_n[span, :], block, preferred_element_type=jnp.float32)
            factor = gain[g * 2 + k, span, :]
            value = factor * (pred + shift[g * 2 + k, span, :])
            smooth = (0.5 * scale) - (0.5 * scale) * jnp.tanh(value)
            slopes.append(jnp.where(factor > 0.0, value, smooth).astype(jnp.bfloat16))
        slope = jnp.concatenate(slopes, axis=0)
        far = jnp.dot(rows_t[...], slope, preferred_element_type=jnp.float32)
        part_own[k, g] = far[:, :piece]
        part_out[k, g] = far[:, piece:]
        send(PART_A + k, g, part_out.at[k, g], part_in.at[k, g], part_sem.at[k, g], core_id)
        row_grad[...] += lax.dot_general(block, slope, (((1,), (1,)), ((), ())), preferred_element_type=jnp.float32)

    def arrived(d, g):
        landed(came.at[d, g], came_sem.at[d, g])

    def pass_first(g):
        arrived(0, g)
        send(TO_CORE, g, came.at[0, g], came.at[1, g], came_sem.at[1, g], core_id)

        def on():
            send(TO_NEAR, g, came.at[0, g], came.at[2, g], came_sem.at[2, g], near_id)

        on() if g < cuts else pl.when(inner)(on)

    def pass_second(g):
        arrived(2, g)
        send(TO_CORE_FAR, g, came.at[2, g], came.at[3, g], came_sem.at[3, g], core_id)
        if g >= cuts:
            @pl.when(inner)
            def _():
                send(TO_NEAR_FAR, g, came.at[2, g], came.at[0, g], came_sem.at[0, g], near_id)

    def chip_sum(g, k):
        landed(part_in.at[k, g], part_sem.at[k, g])
        return part_own[k, g] + part_in[k, g]

    def to_near(g, k):
        near_out[1 - k, g] = chip_sum(g, k).astype(jnp.bfloat16)
        send(SUM_NEAR + 1 - k, g, near_out.at[1 - k, g], near_in.at[1 - k, g], near_sem.at[1 - k, g], near_id)

    def both_sum(g, k):
        own = chip_sum(g, k)
        landed(near_in.at[k, g], near_sem.at[k, g])
        return own + near_in[k, g].astype(jnp.float32)

    def total_first(g):
        later = g + cuts
        total = both_sum(g, 0)
        sent[later] = (came[0, g].astype(jnp.float32) - STEP * total).astype(jnp.bfloat16)

        @pl.when(outer)
        def _():
            send(TO_PARTNER, later, sent.at[later], came.at[0, later], came_sem.at[0, later], both_along_id)

        @pl.when(inner)
        def _():
            send(TO_PARTNER, later, sent.at[later], came.at[2, later], came_sem.at[2, later], both_touch_id)

        total_out[0, g] = total.astype(jnp.bfloat16)
        send(TOTAL, g, total_out.at[0, g], total_in.at[g], total_sem.at[g], across_id)

    def total_last(g):
        total_out[0, g] = both_sum(g, 0).astype(jnp.bfloat16)
        send(TOTAL, g, total_out.at[0, g], total_in.at[g], total_sem.at[g], along_id)
        total_out[1, g] = both_sum(g, 1).astype(jnp.bfloat16)
        send(TOTAL_FAR, g, total_out.at[1, g], total_in.at[g], total_sem.at[g], touch_id)

    def finish(g):
        j = g % cuts
        landed(total_in.at[g], total_sem.at[g])
        spot = slice(j * piece, (j + 1) * piece)
        new = cols_f[:, spot] - STEP * total_in[g].astype(jnp.float32)
        if g < pieces - cuts:
            cols_f[:, spot] = new
        else:
            cols_out[:, spot] = new[:width, :]

    def new_rows():
        rows_f[...] = rows_f[...] - STEP * row_grad[...]
        set_rows()

    def ready(s, carry):
        prepare(s // 2, s % 2)
        return carry

    lax.fori_loop(0, units, ready, 0)

    def ready_more(low, high):
        lax.fori_loop(units + low, units + high, ready, 0)

    ahead = [
        [(pass_first, 0), (arrived, 1, 0)],
        [(pass_first, 1), (arrived, 1, 1)],
        [(pass_first, 2), (pass_second, 0), (arrived, 3, 0)],
        [(arrived, 1, 2)],
        [(pass_first, 3), (pass_second, 1), (arrived, 3, 1)],
        [(to_near, 0, 1), (arrived, 1, 3)],
        [(pass_second, 2), (arrived, 3, 2)],
        [(to_near, 1, 1), (total_first, 0), (pass_second, 3), (arrived, 3, 3)],
        [
            (to_near, 2, 1), (to_near, 3, 1), (new_rows,), (total_first, 1), (ready_more, 0, 3),
            (total_first, 2), (ready_more, 3, 6), (total_first, 3), (ready_more, 6, 8), (pass_first, 4), (pass_second, 4),
            (arrived, 1, 4),
        ],
        [(arrived, 3, 4)],
    ]
    for g in range(cuts + 1, pieces):
        ahead.append(["outer", (to_near, g - 1, 1), (to_near, g - 1, 0), "all", (pass_first, g), (pass_second, g), (arrived, 1, g)])
        if g == cuts + 2:
            ahead[-1] += [(finish, 0), (finish, 1)]
        if g == cuts + 3:
            ahead[-1] += [(finish, 2), (finish, 3)]
        ahead.append([(arrived, 3, g)])

    def act(steps):
        mine, rest = [], []
        for step in steps:
            if step == "outer":
                rest = mine
                mine = []
            elif step == "all":
                todo = mine

                @pl.when(outer)
                def _():
                    for call, *args in todo:
                        call(*args)

                mine = []
            else:
                mine.append(step)
        for call, *args in mine:
            call(*args)

    def body(t, carry):
        rnd, s = t // units, t % units
        k0 = other(s % 2) * ((s + units - 1) // units) + s // (units - 1)
        j0 = (s + 1) // 2 - k0
        j = j0 + rnd * (s // 2 - j0)
        k = k0 + rnd * (s % 2 - k0)
        g = rnd * cuts + j

        for start in range(0, len(ahead), 4):
            @pl.when((t >= start) & (t < start + 4))
            def _():
                for now in range(start, start + 4):
                    pl.when(t == now)(functools.partial(act, ahead[now]))

        compute(g, k)
        return carry

    lax.fori_loop(0, rounds * units, body, 0)

    @pl.when(outer)
    def _():
        to_near(pieces - 1, 1)
        to_near(pieces - 1, 0)

    rows_out[...] = rows_f[:width, :] - STEP * row_grad[:width, :]

    @pl.when(inner)
    def _():
        for g in range(cuts, pieces):
            total_last(g)

    for g in range(cuts, pieces):
        finish(g)

    def sent_off(kind, ref):
        pltpu.make_async_copy(ref, ref, send_sem.at[kind]).wait()

    half = sent.at[:cuts]
    for kind in (TO_PARTNER, TO_CORE, TO_CORE_FAR):
        sent_off(kind, sent)
    for kind in (PART_A, PART_B):
        sent_off(kind, part_out.at[0])

    @pl.when(inner)
    def _():
        for kind, ref in ((TO_NEAR, sent), (TOTAL, sent), (TO_NEAR_FAR, half), (TOTAL_FAR, half), (SUM_NEAR, half)):
            sent_off(kind, ref)

    @pl.when(outer)
    def _():
        for kind, ref in ((TO_NEAR, half), (TOTAL, half), (SUM_NEAR, sent), (SUM_NEAR_FAR, half)):
            sent_off(kind, ref)


def settle(rows_ref, cols_ref, rows_out, cols_out, sem):
    copies = [
        pltpu.make_async_copy(rows_ref, rows_out, sem.at[0]),
        pltpu.make_async_copy(cols_ref, cols_out, sem.at[1]),
    ]
    for copy in copies:
        copy.start()
    for copy in copies:
        copy.wait()


def solution(mesh):
    n_blk = mesh.shape["blk"]

    def per_device(row_embed, col_embed, counts, log_marginal):
        local, width = row_embed.shape
        rounds = counts.shape[0]
        padded = -(-width // 16) * 16
        piece = local // CUTS
        pieces = rounds * CUTS
        vmem = pltpu.VMEM
        f32, half = jnp.float32, jnp.bfloat16
        block = (padded, piece)
        rows_t, cols_t = pl.pallas_call(
            functools.partial(kernel, n_blk, rounds, CUTS, piece),
            out_shape=[jax.ShapeDtypeStruct((width, local), f32)] * 2,
            in_specs=[
                pl.BlockSpec(memory_space=pl.ANY),
                pl.BlockSpec(memory_space=pl.ANY),
                pl.BlockSpec(memory_space=pl.ANY),
                pl.BlockSpec(memory_space=pl.ANY),
            ],
            out_specs=[pl.BlockSpec(memory_space=vmem)] * 2,
            scratch_shapes=[
                vmem((rounds * PARTS, local, local), jnp.int32),
                vmem((pieces * 2, local, 2 * piece), f32),
                vmem((pieces * 2, local, 2 * piece), f32),
                vmem((padded, local), f32),
                vmem((padded, local), half),
                vmem((local, padded), half),
                vmem((padded, local), f32),
                vmem((padded, local), f32),
                vmem((local, 128), f32),
                vmem((pieces,) + block, half),
                vmem((PARTS, pieces) + block, half),
                vmem((2, pieces) + block, f32),
                vmem((2, pieces) + block, f32),
                vmem((2, pieces) + block, f32),
                vmem((2, pieces) + block, half),
                vmem((2, pieces) + block, half),
                vmem((2, pieces) + block, half),
                vmem((pieces,) + block, half),
                vmem((local * PARTS * n_blk // 128, 128), f32),
                vmem((width, local), f32),
                vmem((width, local), f32),
                pltpu.SemaphoreType.DMA((3,)),
                pltpu.SemaphoreType.DMA((rounds * PARTS,)),
                pltpu.SemaphoreType.DMA((KINDS,)),
                pltpu.SemaphoreType.DMA((PARTS, pieces)),
                pltpu.SemaphoreType.DMA((2, pieces)),
                pltpu.SemaphoreType.DMA((2, pieces)),
                pltpu.SemaphoreType.DMA((pieces,)),
            ],
            compiler_params=pltpu.CompilerParams(
                collective_id=0, has_side_effects=True, vmem_limit_bytes=52 * 2**20
            ),
        )(row_embed.T, col_embed.T, counts, log_marginal.reshape(-1, 128))
        rows_t, cols_t = pl.pallas_call(
            settle,
            out_shape=[jax.ShapeDtypeStruct((width, local), f32)] * 2,
            in_specs=[pl.BlockSpec(memory_space=pl.ANY)] * 2,
            out_specs=[pl.BlockSpec(memory_space=pl.ANY)] * 2,
            scratch_shapes=[pltpu.SemaphoreType.DMA((2,))],
            compiler_params=pltpu.CompilerParams(vmem_limit_bytes=2**20),
        )(rows_t, cols_t)
        return rows_t.T, cols_t.T

    placed = (P(("blk", "rep"), None), P(("blk", "rep"), None), P(None, ("blk", "rep"), None), P())
    return jax.shard_map(
        per_device,
        mesh=mesh,
        in_specs=placed,
        out_specs=(P(("blk", "rep"), None), P(("blk", "rep"), None)),
        check_vma=False,
    )
```
